32 devices in a mesh: dp: 4 (over y, core), expert: 8 (over z, x).
Axes of the slice: x: 2, y: 2, z: 4, core: 2. Of those that a mesh axis runs over, the one named last changes fastest.
Arguments:
- tokens: bfloat16 [4096, 2048], P(('dp', 'expert')), may hold values from -6 to 6
- out_grad: bfloat16 [4096, 2048], P(('dp', 'expert')), may hold values from -6 to 6
- route_ids: int32 [4096, 2], P(('dp', 'expert')), may hold values from 0 to 7, as said below
- route_gates: bfloat16 [4096, 2], P(('dp', 'expert')), may hold values from 0.049804688 to 1
- weight_in: bfloat16 [8, 2048, 512], P('expert', 'dp'), may hold values from -0.125 to 0.125
- weight_out: bfloat16 [8, 512, 2048], P('expert', None, 'dp'), may hold values from -0.25 to 0.25
Outputs:
- grad_tokens: bfloat16 [4096, 2048], P(('dp', 'expert'))
- grad_gates: bfloat16 [4096, 2], P(('dp', 'expert'))
- grad_weight_in: float32 [8, 2048, 512], P('expert', 'dp')
- grad_weight_out: float32 [8, 512, 2048], P('expert', None, 'dp')
The draws below stay inside these ranges and needn't reach their ends.
Inputs may be any that keep to these rules, and one draw needn't show every extreme that they name: `route_ids`: each row names two different experts. Within the 128 tokens of one device (aligned blocks of 128 rows), every expert is named by at most 64 rows. For each index of dp, one expert is named by exactly 64 rows in every block of that index's 1024 rows.
All inputs are finite; a program needn't handle non-finite values.
Results may differ from the reference program's by a relative error of at most 0.017.
Values may be sent and summed in bfloat16 or wider, within the bound.
No kernel may reach another device: no remote copies, remote signals or barrier semaphores. Data moves between devices by JAX's collectives and lax.ppermute only.
A program may use at most 64 MiB of HBM per device.

```python
import jax
import jax.numpy as jnp
from jax import lax

D = 2048
H = 512
TOK_DEV = 128
EXPERTS = 8
CAP = 64
TOKENS = 4096
N_DP = 4
N_EXPERT = 8


def draw_route_ids(key, part):
    blocks = N_DP * N_EXPERT
    capacity = 4 * TOK_DEV // N_EXPERT
    half_experts = N_EXPERT // 2
    jitter_width = capacity // 8
    row_keys = jax.random.split(jax.random.fold_in(key, 11), N_DP)

    def row_plan(row_key):
        expert_order = jax.random.permutation(jax.random.fold_in(row_key, 1), N_EXPERT).astype(jnp.int32)
        base_split = jax.random.randint(jax.random.fold_in(row_key, 2), (half_experts,), 0, capacity + 1)
        base_split = base_split.at[0].set(capacity)
        return (expert_order, base_split.astype(jnp.int32))
    orders, bases = jax.vmap(row_plan)(row_keys)
    device_keys = jax.random.split(jax.random.fold_in(key, 12), blocks)

    def block_ids(device_key, expert_order, base_split):
        jitter = jax.random.randint(jax.random.fold_in(device_key, 1), (half_experts,), -jitter_width, jitter_width + 1)
        jitter = jitter.at[0].set(0)
        split_count = jnp.clip(base_split + jitter.astype(jnp.int32), 0, capacity)
        count_by_rank = jnp.concatenate([split_count, capacity - split_count])
        counts = jnp.zeros((N_EXPERT,), jnp.int32).at[expert_order].set(count_by_rank)
        count_ends = jnp.cumsum(counts)
        position = jnp.arange(2 * TOK_DEV, dtype=jnp.int32)
        labels = jnp.sum((position[:, None] >= count_ends[None, :]).astype(jnp.int32), axis=1)
        pair_ids = jnp.stack([labels[:TOK_DEV], labels[TOK_DEV:]], axis=1)
        swap_bits = jax.random.randint(jax.random.fold_in(device_key, 3), (TOK_DEV, 1), 0, 2)
        pair_ids = jnp.where(swap_bits > 0, pair_ids[:, ::-1], pair_ids)
        row_order = jax.random.permutation(jax.random.fold_in(device_key, 2), TOK_DEV)
        return pair_ids[row_order]
    order_rep = jnp.repeat(orders, N_EXPERT, axis=0)
    base_rep = jnp.repeat(bases, N_EXPERT, axis=0)
    all_ids = jax.vmap(block_ids)(device_keys, order_rep, base_rep)
    return all_ids.reshape(TOKENS, 2).astype(jnp.int32)


def block_scale(rng, shape, cuts, smallest, top_value):
    factor_of = 1.0
    for dim, shards_of in cuts:
        draws = jax.random.uniform(jax.random.fold_in(jax.random.fold_in(rng, 6), dim), (shards_of,), jnp.float32, smallest / len(cuts), top_value / len(cuts))
        factor_of = factor_of * jnp.repeat(jnp.exp(draws), shape[dim] // shards_of).reshape((-1,) + (1,) * (len(shape) - 1 - dim))
    return factor_of


def centred(own_key, shape, spread, limit, cuts=(), kind=jnp.bfloat16):
    gain = block_scale(own_key, shape, cuts, -0.22, 0.18) if cuts else 1.0
    values = jax.random.normal(own_key, shape, jnp.float32) * spread * gain
    return jnp.minimum(jnp.maximum(values, -limit), limit).astype(kind)


def setup_inputs(seed: int = 0) -> dict:
    seeds = jax.random.split(jax.random.key(seed), 7)
    return {
        "tokens": centred(seeds[0], (TOKENS, D), 1.0, 6.0, ((0, 32),)),
        "out_grad": centred(seeds[1], (TOKENS, D), 1.0, 6.0, ((0, 32),)),
        "route_ids": draw_route_ids(jax.random.fold_in(seeds[6], 71), 0),
        "route_gates": jnp.clip(0.049804688 + 0.9501953 * jax.random.uniform(seeds[3], (TOKENS, 2), jnp.float32) ** block_scale(seeds[3], (TOKENS, 2), ((0, 32),), -0.2, 0.2), 0.049804688, 1.0).astype(jnp.bfloat16),
        "weight_in": centred(seeds[4], (EXPERTS, D, H), D ** -0.5, 0.125, ((0, 8), (1, 4))),
        "weight_out": centred(seeds[5], (EXPERTS, H, D), H ** -0.5, 0.25, ((0, 8), (2, 4))),
    }


def silu_slope(preact):
    logistic = jax.nn.sigmoid(preact)
    return logistic * (1.0 + preact * (1.0 - logistic))


def reference(tokens, out_grad, route_ids, route_gates, weight_in, weight_out):
    experts = weight_in.shape[0]
    blocks = N_DP * N_EXPERT
    capacity = CAP
    routes = 2 * TOKENS
    block_ids = route_ids.reshape(blocks, 2 * TOK_DEV).astype(jnp.int32)
    onehot = (block_ids[:, :, None] == jnp.arange(experts, dtype=jnp.int32)[None, None, :]).astype(jnp.int32)
    route_rank = jnp.sum(jnp.cumsum(onehot, axis=1) * onehot, axis=2) - 1
    block_number = jnp.arange(blocks, dtype=jnp.int32)[:, None]
    position = ((block_ids * blocks + block_number) * capacity + route_rank).reshape(-1).astype(jnp.int32)
    slot_table = jnp.full((experts * blocks * capacity,), routes, jnp.int32)
    slot_table = slot_table.at[position].set(jnp.arange(routes, dtype=jnp.int32))
    slot_table = slot_table.reshape(experts, N_DP, N_EXPERT * capacity)
    gate_flat = route_gates.reshape(-1)
    group_shape = (N_DP, N_EXPERT * capacity)

    def one_expert(loop_state, expert_data):
        token_sum, gate_out = loop_state
        expert_rows, proj_in, proj_out = expert_data
        flat_rows = expert_rows.reshape(-1)
        token_index = (flat_rows // 2).astype(jnp.int32)
        inputs = jnp.take(tokens, token_index, axis=0, mode="fill", fill_value=0)
        grad_rows = jnp.take(out_grad, token_index, axis=0, mode="fill", fill_value=0)
        gate_rows = jnp.take(gate_flat, flat_rows, axis=0, mode="fill", fill_value=0)
        preact = jnp.dot(inputs, proj_in, preferred_element_type=jnp.float32)
        hidden_act = jax.nn.silu(preact).astype(jnp.bfloat16)
        back_grad = jnp.dot(grad_rows, proj_out.T, preferred_element_type=jnp.float32)
        weight = gate_rows.astype(jnp.float32)[:, None]
        gate_grad = jnp.sum(hidden_act.astype(jnp.float32) * back_grad, axis=1).astype(jnp.bfloat16)
        pre_grad = (weight * back_grad * silu_slope(preact)).astype(jnp.bfloat16)
        scaled = (weight * grad_rows.astype(jnp.float32)).astype(jnp.bfloat16)
        route_grad = jnp.dot(pre_grad, proj_in.T, preferred_element_type=jnp.float32).astype(jnp.bfloat16)
        token_sum = token_sum.at[token_index].add(route_grad.astype(token_sum.dtype), mode="drop")
        gate_out = gate_out.at[flat_rows].set(gate_grad, mode="drop")
        width = inputs.shape[1]
        hidden = preact.shape[1]
        part_in = jnp.einsum("gsd,gsh->gdh", inputs.reshape(group_shape + (width,)).astype(jnp.float32),
                             pre_grad.reshape(group_shape + (hidden,)).astype(jnp.float32)).astype(jnp.bfloat16)
        part_out = jnp.einsum("gsh,gsd->ghd", hidden_act.reshape(group_shape + (hidden,)).astype(jnp.float32),
                              scaled.reshape(group_shape + (width,)).astype(jnp.float32)).astype(jnp.bfloat16)
        grad_in = jnp.sum(part_in.astype(jnp.float32), axis=0)
        grad_out = jnp.sum(part_out.astype(jnp.float32), axis=0)
        return (token_sum, gate_out), (grad_in, grad_out)

    initial = (jnp.zeros((TOKENS, tokens.shape[1]), jnp.float32), jnp.zeros((routes,), jnp.bfloat16))
    (token_sum, gate_out), (grad_weight_in, grad_weight_out) = lax.scan(
        one_expert, initial, (slot_table, weight_in, weight_out))
    grad_tokens = token_sum.astype(jnp.bfloat16)
    grad_gates = gate_out.reshape(TOKENS, 2)
    return grad_tokens, grad_gates, grad_weight_in, grad_weight_out
```

```python
import jax
import jax.numpy as jnp
from jax import lax
from jax.sharding import PartitionSpec as P

BF16 = jnp.bfloat16
F32 = jnp.float32


def swap(value, axis, bit):
    return lax.ppermute(value, axis, [(i, i ^ bit) for i in range(lax.axis_size(axis))])


def bits_of(count):
    return [1 << b for b in reversed(range(count.bit_length() - 1))]


def relative_columns(value, index, parts):
    rows, width = value.shape
    for bit in bits_of(parts):
        span = bit * (width // parts)
        halves = value.reshape(rows, width // (2 * span), 2, span)
        value = jnp.where((index & bit) != 0, halves[:, :, ::-1], halves).reshape(rows, width)
    return value


def plus(a, b):
    return (a.astype(F32) + b.astype(F32)).astype(BF16)


def dot(a, b, ca, cb):
    return lax.dot_general(a, b, (((ca,), (cb,)), ((), ())), preferred_element_type=F32)


def on_device(tokens, out_grad, route_ids, route_gates, weight_in, weight_out):
    local_tokens, model_width = tokens.shape
    experts = lax.axis_size("expert")
    slices = lax.axis_size("dp")
    hidden = weight_in.shape[2]
    me_e = lax.axis_index("expert")
    me_d = lax.axis_index("dp")

    share = experts // 4
    token_bits = [b for b in bits_of(experts) if b != share]
    dp_bits = bits_of(slices)

    tok = {0: relative_columns(tokens, me_d, slices)}
    grd = {0: relative_columns(out_grad, me_d, slices)}
    for bit in token_bits:
        for held in (tok, grd):
            for m in list(held):
                held[m | bit] = swap(held[m], "expert", bit)

    shard = jnp.stack([weight_in[0], weight_out[0].T])
    pieces = {(0, 0): shard, (1, 0): swap(shard, "expert", share)}
    for bit in dp_bits:
        for s, m in list(pieces):
            pieces[s, m | bit] = swap(pieces[s, m], "dp", bit)
    order = sorted(tok)
    half = len(order) // 2
    near, far = order[:half], order[half:]

    def whole(which):
        return jnp.concatenate(
            [
                jnp.concatenate([pieces[s, m][which] for m in range(slices)], axis=0)
                for s in range(2)
            ],
            axis=1,
        )

    full_in = whole(0)
    full_out = whole(1)

    chosen = route_ids[None] == jnp.arange(experts, dtype=jnp.int32)[:, None, None]
    gate_table = jnp.sum(jnp.where(chosen, route_gates[None].astype(F32), 0.0), axis=2).astype(BF16)
    all_gates = lax.all_gather(gate_table, "expert", axis=0)
    block_of = me_e ^ jnp.array(order, jnp.int32)
    expert_of = me_e ^ jnp.array([0, share], jnp.int32)
    my_gates = all_gates[block_of][:, expert_of].astype(F32)

    def rows(held, part):
        return jnp.concatenate([held[m] for m in part], axis=0)

    def run(part):
        first = order.index(part[0])
        gates = my_gates[first : first + len(part)]
        gates = gates.transpose(0, 2, 1).reshape(len(part) * local_tokens, 2)
        gates = jnp.repeat(gates, hidden, axis=1)
        t, g = rows(tok, part), rows(grd, part)
        preact = dot(t, full_in, 1, 0)
        back = dot(g, full_out, 1, 0)
        logistic = jax.nn.sigmoid(preact)
        act = preact * logistic
        slope = logistic * (1.0 + preact * (1.0 - logistic))
        pre_grad = (gates * back * slope).astype(BF16)
        scaled_act = (gates * act).astype(BF16)
        product = act.astype(BF16).astype(F32) * back
        gate_grad = jnp.sum(product.reshape(-1, 2, hidden), axis=2)
        return t, g, pre_grad, scaled_act, gate_grad

    near_t, near_g, near_pre, near_act, near_gg = run(near)
    far_t, far_g, far_pre, far_act, far_gg = run(far)

    route = {}
    for part, pre in ((far, far_pre), (near, near_pre)):
        out = dot(pre, full_in, 1, 1).astype(BF16)
        for i, m in enumerate(part):
            route[m] = out[i * local_tokens : (i + 1) * local_tokens]
    for bit in reversed(token_bits):
        for m in sorted(route, reverse=True):
            if m & bit:
                route[m ^ bit] = plus(route[m ^ bit], swap(route.pop(m), "expert", bit))
    grad_tokens = relative_columns(route[0], me_d, slices)

    gate_grad = jnp.concatenate([near_gg, far_gg], axis=0).T.astype(BF16)
    gate_grad = gate_grad.reshape(2, len(order), local_tokens)
    all_gate_grads = lax.all_gather(gate_grad, "expert", axis=0)
    expert_ids = jnp.arange(experts, dtype=jnp.int32)
    worker = (expert_ids & ~share) | (me_e & share)
    slot = ((expert_ids ^ worker) != 0).astype(jnp.int32)
    rank = jnp.sum((worker ^ me_e)[:, None] > jnp.array(order, jnp.int32)[None], axis=1)
    by_expert = all_gate_grads[worker, slot, rank].astype(F32)
    grad_gates = jnp.sum(jnp.where(chosen, by_expert[:, :, None], 0.0), axis=0).astype(BF16)

    all_t = jnp.concatenate([near_t, far_t], axis=0)
    all_g = jnp.concatenate([near_g, far_g], axis=0)
    all_pre = jnp.concatenate([near_pre, far_pre], axis=0)
    all_act = jnp.concatenate([near_act, far_act], axis=0)
    part_in = dot(all_t, all_pre, 0, 0).astype(BF16).reshape(slices, -1, 2, hidden)
    part_out = dot(all_act, all_g, 0, 0).astype(BF16).reshape(2, hidden, slices, -1)
    in_sum = {(s, m): part_in[m, :, s] for s in range(2) for m in range(slices)}
    out_sum = {(s, m): part_out[s, :, m] for s in range(2) for m in range(slices)}

    def fold_dp(held, bit, total=plus):
        sent = sorted(k for k in held if k[1] & bit)
        came = swap(jnp.stack([held.pop(k) for k in sent]), "dp", bit)
        for i, (s, m) in enumerate(sent):
            held[s, m ^ bit] = total(held[s, m ^ bit], came[i])

    def fold_share(held, total=plus):
        sent = sorted(k for k in held if k[0])
        came = swap(jnp.stack([held.pop(k) for k in sent]), "expert", share)
        for i, (s, m) in enumerate(sent):
            held[0, m] = total(held[0, m], came[i])

    def wide(a, b):
        return a.astype(F32) + b.astype(F32)

    core, others = dp_bits[-1], dp_bits[:-1]
    fold_dp(in_sum, core)
    fold_dp(out_sum, core)
    fold_share(in_sum)
    for bit in others:
        fold_dp(out_sum, bit)
    for bit in others:
        fold_dp(in_sum, bit, wide if bit == others[-1] else plus)
    fold_share(out_sum, wide)
    return (
        grad_tokens,
        grad_gates,
        in_sum[0, 0][None],
        out_sum[0, 0][None],
    )


def solution(mesh):
    return jax.shard_map(
        on_device,
        mesh=mesh,
        in_specs=(
            P(("dp", "expert"), None),
            P(("dp", "expert"), None),
            P(("dp", "expert"), None),
            P(("dp", "expert"), None),
            P("expert", "dp", None),
            P("expert", None, "dp"),
        ),
        out_specs=(
            P(("dp", "expert"), None),
            P(("dp", "expert"), None),
            P("expert", "dp", None),
            P("expert", None, "dp"),
        ),
        check_vma=False,
    )
```

```python
import functools

import jax
import jax.numpy as jnp
from jax import lax
from jax.experimental import pallas as pl
from jax.experimental.pallas import tpu as pltpu
from jax.sharding import PartitionSpec as P

BF16 = jnp.bfloat16
F32 = jnp.float32
VMEM_LIMIT = 50 * 1024 * 1024
TILE = 256


def swap(value, axis, bit):
    return lax.ppermute(value, axis, [(i, i ^ bit) for i in range(lax.axis_size(axis))])


def bits_of(count):
    return [1 << b for b in reversed(range(count.bit_length() - 1))]


def plus(a, b):
    return (a.astype(F32) + b.astype(F32)).astype(BF16)


def wide(a, b):
    return a.astype(F32) + b.astype(F32)


def dot(a, b, ca=1, cb=0):
    return lax.dot_general(a, b, (((ca,), (cb,)), ((), ())), preferred_element_type=F32)


ANY = pl.BlockSpec(memory_space=pl.ANY)
VMEM = pl.BlockSpec(memory_space=pltpu.VMEM)
SMEM = pl.BlockSpec(memory_space=pltpu.SMEM)


def call(body, name, in_specs, out_shape, scratch, flops, moved):
    return pl.pallas_call(
        body,
        name=name,
        in_specs=in_specs,
        out_specs=[VMEM] * len(out_shape),
        out_shape=out_shape,
        scratch_shapes=scratch,
        compiler_params=pltpu.CompilerParams(vmem_limit_bytes=VMEM_LIMIT),
        cost_estimate=pl.CostEstimate(flops=flops, bytes_accessed=moved, transcendentals=0),
    )


def shape(*dims, dtype=BF16):
    return jax.ShapeDtypeStruct(dims, dtype)


class Copies:
    def __init__(self, sems):
        self.sems = sems
        self.count = 0

    def start(self, src, dst):
        copy = pltpu.make_async_copy(src, dst, self.sems.at[self.count])
        self.count += 1
        copy.start()
        return copy


def prepare_body(ids, gates, weight_in, weight_out, table, stack):
    lanes = lax.broadcasted_iota(jnp.int32, table.shape, 1)
    total = jnp.zeros(table.shape, F32)
    for k in range(2):
        total += jnp.where(lanes == ids[:, k : k + 1], gates[:, k : k + 1].astype(F32), 0.0)
    table[...] = total.astype(BF16)
    stack[0] = weight_in[0]
    stack[1] = weight_out[0].T


def start_rows(copies, blocks, dst):
    rows = blocks[0].shape[0]
    return [copies.start(b, dst.at[pl.ds(i * rows, rows)]) for i, b in enumerate(blocks)]


def start_weights(copies, pieces, which, me_d, dst):
    depth = dst.shape[1] // (len(pieces) // 2)
    started = {0: [], 1: []}
    for (s, m), ref in sorted(pieces.items()):
        place = pl.multiple_of((me_d ^ m) * depth, depth)
        started[s].append(copies.start(ref.at[which], dst.at[s, pl.ds(place, depth)]))
    return started


def wait(copies):
    for copy in copies:
        copy.wait()


def forward_body(blocks, keys, share, *refs):
    place, refs = refs[0], refs[1:]
    tok, refs = refs[:blocks], refs[blocks:]
    tables, refs = refs[:blocks], refs[blocks:]
    pieces, refs = dict(zip(keys, refs)), refs[len(keys) :]
    hid, slope_out, act_t, tok_t, t, w, sems = refs
    me_e, me_d = place[0], place[1]
    copies = Copies(sems)
    rows_in = start_rows(copies, tok, t)
    weights_in = start_weights(copies, pieces, 0, me_d, w)
    lanes = lax.broadcasted_iota(jnp.int32, tables[0].shape, 1)

    def gate_of(s):
        e = me_e ^ (share * s)
        columns = [
            jnp.sum(jnp.where(lanes == e, tb[...].astype(F32), 0.0), axis=1, keepdims=True)
            for tb in tables
        ]
        return jnp.concatenate(columns, axis=0)

    gates = [gate_of(s) for s in range(2)]
    wait(rows_in)
    width, hidden = w.shape[1:]

    @pl.loop(0, width // TILE)
    def _(j):
        at = pl.ds(pl.multiple_of(j * TILE, TILE), TILE)
        tok_t[at, :] = t[:, at].T

    for s in range(2):
        wait(weights_in[s])

        @pl.loop(0, hidden // TILE)
        def _(j, s=s):
            at = pl.ds(pl.multiple_of(j * TILE, TILE), TILE)
            to = pl.ds(pl.multiple_of(s * hidden + j * TILE, TILE), TILE)
            preact = dot(t[...], w[s, :, at])
            logistic = jax.nn.sigmoid(preact)
            act = preact * logistic
            hid[:, to] = act.astype(BF16)
            slope_out[:, to] = (gates[s] * (logistic * (1.0 + preact * (1.0 - logistic)))).astype(BF16)
            act_t[to, :] = (gates[s] * act).astype(BF16).T


def backward_body(blocks, keys, share, order, *refs):
    place, refs = refs[0], refs[1:]
    grd, refs = refs[:blocks], refs[blocks:]
    pieces, refs = dict(zip(keys, refs)), refs[len(keys) :]
    hid, slope, tok_t, pre, table, keep, send, g, w, sems = refs
    me_e, me_d = place[0], place[1]
    copies = Copies(sems)
    weights_in = start_weights(copies, pieces, 1, me_d, w)
    rows_in = start_rows(copies, grd, g)
    width, hidden = w.shape[1:]
    rows = g.shape[0]
    depth = keep.shape[1]
    wait(rows_in)
    columns = {}
    for s in (1, 0):
        wait(weights_in[s])

        def step(j, total, s=s):
            at = pl.ds(pl.multiple_of(j * TILE, TILE), TILE)
            to = pl.ds(pl.multiple_of(s * hidden + j * TILE, TILE), TILE)
            back = dot(g[...], w[s, :, at])
            pre[:, to] = (slope[:, to].astype(F32) * back).astype(BF16)
            return total + jnp.sum(hid[:, to].astype(F32) * back, axis=1, keepdims=True)

        columns[s] = lax.fori_loop(0, hidden // TILE, step, jnp.zeros((rows, 1), F32))
        if s:

            @pl.loop(0, width // depth // 2)
            def _(j, s=s):
                for out, core in ((keep, 0), (send, 1)):
                    at = pl.ds(pl.multiple_of((me_d ^ (2 * j + core)) * depth, depth), depth)
                    out[j] = dot(tok_t[at, :], pre[:, s * hidden :]).astype(BF16)

    lanes = lax.broadcasted_iota(jnp.int32, (rows, table.shape[1]), 1)
    total = jnp.zeros(lanes.shape, F32)
    for s in range(2):
        total += jnp.where(lanes == me_e ^ (share * s), columns[s], 0.0)
    table[...] = total.astype(BF16)


def route_body(blocks, keys, first, *refs):
    place, refs = refs[0], refs[1:]
    pieces, refs = dict(zip(keys, refs)), refs[len(keys) :]
    source, refs = refs[0], refs[1:]
    outs, (w, pre, sems) = refs[:blocks], refs[blocks:]
    copies = Copies(sems)
    wait([copies.start(source.at[pl.ds(first, pre.shape[0])], pre)])
    weights_in = start_weights(copies, pieces, 0, place[1], w)
    wait(weights_in[0])
    wait(weights_in[1])
    width, hidden = w.shape[1:]
    rows = outs[0].shape[0]

    @pl.loop(0, width // TILE)
    def _(j):
        at = pl.ds(pl.multiple_of(j * TILE, TILE), TILE)
        total = dot(pre[:, :hidden], w[0, at, :], 1, 1) + dot(pre[:, hidden:], w[1, at, :], 1, 1)
        for i, out in enumerate(outs):
            out[:, at] = total[i * rows : (i + 1) * rows].astype(BF16)


def out_body(blocks, masks, *refs):
    place, refs = refs[0], refs[1:]
    grd, refs = refs[:blocks], refs[blocks:]
    act_t, keep, send, g, sems = refs
    me_d = place[1]
    hidden, depth = keep.shape[2:]
    rows = grd[0].shape[0]
    copies = Copies(sems)
    started = {}
    for n, m in enumerate(masks):
        for core in range(2):
            at = pl.ds(pl.multiple_of((me_d ^ (m | core)) * depth, depth), depth)
            started[n, core] = [
                copies.start(b.at[:, at], g.at[2 * n + core, pl.ds(i * rows, rows)])
                for i, b in enumerate(grd)
            ]
    for n, m in enumerate(masks):
        for core, out in ((1, send), (0, keep)):
            wait(started[n, core])
            for s in range(2):
                out[s, n] = dot(act_t[s * hidden : (s + 1) * hidden, :], g[2 * n + core]).astype(BF16)


def in_body(*refs):
    place, tok_t, pre, keep, send = refs
    me_d = place[1]
    depth = keep.shape[1]

    @pl.loop(0, keep.shape[0])
    def _(j):
        for out, core in ((send, 1), (keep, 0)):
            at = pl.ds(pl.multiple_of((me_d ^ (2 * j + core)) * depth, depth), depth)
            out[j] = dot(tok_t[at, :], pre[:, : keep.shape[2]]).astype(BF16)


def on_device(tokens, out_grad, route_ids, route_gates, weight_in, weight_out):
    local, width = tokens.shape
    experts = lax.axis_size("expert")
    slices = lax.axis_size("dp")
    hidden, depth = weight_in.shape[2], weight_in.shape[1]
    place = jnp.stack([lax.axis_index("expert"), lax.axis_index("dp")]).astype(jnp.int32)

    share = experts // 4
    token_bits = [b for b in bits_of(experts) if b != share]
    dp_bits = bits_of(slices)
    core, others = dp_bits[-1], dp_bits[:-1]

    table, shard = call(
        prepare_body,
        "prepare",
        [VMEM] * 4,
        [shape(local, experts), shape(2, depth, hidden)],
        [],
        0,
        4 * depth * hidden * 2,
    )(route_ids, route_gates, weight_in, weight_out)

    tok, grd, gate = {0: tokens}, {0: out_grad}, {0: table}
    for held in (tok, grd, gate):
        for bit in token_bits:
            for m in list(held):
                held[m | bit] = swap(held[m], "expert", bit)
    order = sorted(tok)
    blocks = len(order)
    rows = blocks * local

    pieces = {(0, 0): shard, (1, 0): swap(shard, "expert", share)}
    for bit in dp_bits:
        for s, m in list(pieces):
            pieces[s, m | bit] = swap(pieces[s, m], "dp", bit)
    keys = sorted(pieces)
    weights = [pieces[k] for k in keys]
    product = 2 * rows * width * hidden

    hid, slope, act_t, tok_t = call(
        functools.partial(forward_body, blocks, keys, share),
        "forward",
        [SMEM] + [ANY] * blocks + [VMEM] * blocks + [ANY] * len(keys),
        [
            shape(rows, 2 * hidden),
            shape(rows, 2 * hidden),
            shape(2 * hidden, rows),
            shape(width, rows),
        ],
        [
            pltpu.VMEM((rows, width), BF16),
            pltpu.VMEM((2, width, hidden), BF16),
            pltpu.SemaphoreType.DMA((blocks + len(keys),)),
        ],
        2 * product,
        4 * rows * width + 4 * width * hidden + 12 * rows * hidden,
    )(place, *[tok[m] for m in order], *[gate[m] for m in order], *weights)

    half = slices // 2
    pre, back_table, in_keep, in_send = call(
        functools.partial(backward_body, blocks, keys, share, order),
        "backward",
        [SMEM] + [ANY] * blocks + [ANY] * len(keys) + [VMEM] * 3,
        [
            shape(rows, 2 * hidden),
            shape(rows, experts),
            shape(half, depth, hidden),
            shape(half, depth, hidden),
        ],
        [
            pltpu.VMEM((rows, width), BF16),
            pltpu.VMEM((2, width, hidden), BF16),
            pltpu.SemaphoreType.DMA((blocks + len(keys),)),
        ],
        3 * product,
        4 * rows * width + 6 * width * hidden + 12 * rows * hidden,
    )(place, *[grd[m] for m in order], *weights, hid, slope, tok_t)

    def route_of(part):
        n = len(part)
        first = order.index(part[0]) * local
        outs = call(
            functools.partial(route_body, n, keys, first),
            "route",
            [SMEM] + [ANY] * (len(keys) + 1),
            [shape(local, width)] * n,
            [
                pltpu.VMEM((2, width, hidden), BF16),
                pltpu.VMEM((n * local, 2 * hidden), BF16),
                pltpu.SemaphoreType.DMA((len(keys) + 1,)),
            ],
            2 * product * n // blocks,
            4 * width * hidden + 2 * n * local * (width + 2 * hidden),
        )(place, *weights, pre)
        return dict(zip(part, outs))

    def out_of(masks):
        n = len(masks)
        return call(
            functools.partial(out_body, blocks, masks),
            "partial_out",
            [SMEM] + [ANY] * blocks + [VMEM],
            [shape(2, n, hidden, depth)] * 2,
            [
                pltpu.VMEM((2 * n, rows, depth), BF16),
                pltpu.SemaphoreType.DMA((2 * n * blocks,)),
            ],
            product,
            3 * rows * width,
        )(place, *[grd[m] for m in order], act_t)

    masks = list(range(0, slices, 2))
    high, low = masks[half // 2 :], masks[: half // 2]

    in_far = plus(in_keep, swap(in_send, "dp", core))
    in_far = swap(in_far, "expert", share)
    keep_high, send_high = out_of(high)
    out_far = plus(keep_high, swap(send_high, "dp", core))
    out_far = swap(out_far, "dp", others[0])

    route = route_of(order[blocks // 2 :])
    route.update(route_of(order[: blocks // 2]))
    home = dict(zip(order, jnp.split(back_table, blocks, axis=0)))
    for bit in reversed(token_bits):
        for m in sorted(route, reverse=True):
            if m & bit:
                route[m ^ bit] = plus(route[m ^ bit], swap(route.pop(m), "expert", bit))
                home[m ^ bit] = plus(home[m ^ bit], swap(home.pop(m), "expert", bit))
    grad_tokens = route[0]
    chosen = route_ids[:, :, None] == jnp.arange(experts, dtype=jnp.int32)
    grad_gates = jnp.sum(jnp.where(chosen, home[0].astype(F32)[:, None, :], 0.0), axis=2)

    keep_low, send_low = out_of(low)
    out_sum = plus(keep_low, swap(send_low, "dp", core))
    out_sum = plus(out_sum, out_far)
    for bit in others[1:]:
        n = out_sum.shape[1] // 2
        out_sum = plus(out_sum[:, :n], swap(out_sum[:, n:], "dp", bit))
    grad_out = wide(out_sum[0, 0], swap(out_sum[1, 0], "expert", share))

    in_keep, in_send = call(
        in_body,
        "partial_in",
        [SMEM, VMEM, VMEM],
        [shape(half, depth, hidden)] * 2,
        [],
        product,
        3 * rows * width,
    )(place, tok_t, pre)
    in_sum = plus(in_keep, swap(in_send, "dp", core))
    in_sum = plus(in_sum, in_far)
    for bit in others:
        n = in_sum.shape[0] // 2
        total = wide if bit == others[-1] else plus
        in_sum = total(in_sum[:n], swap(in_sum[n:], "dp", bit))
    return (grad_tokens, grad_gates.astype(BF16), in_sum, grad_out[None])


def solution(mesh):
    return jax.shard_map(
        on_device,
        mesh=mesh,
        in_specs=(
            P(("dp", "expert"), None),
            P(("dp", "expert"), None),
            P(("dp", "expert"), None),
            P(("dp", "expert"), None),
            P("expert", "dp", None),
            P("expert", None, "dp"),
        ),
        out_specs=(
            P(("dp", "expert"), None),
            P(("dp", "expert"), None),
            P("expert", "dp", None),
            P("expert", None, "dp"),
        ),
        check_vma=False,
    )
```

```python
import functools

import jax
import jax.numpy as jnp
from jax import lax
from jax.experimental import pallas as pl
from jax.experimental.pallas import tpu as pltpu
from jax.sharding import PartitionSpec as P

BF16 = jnp.bfloat16
F32 = jnp.float32
VMEM_LIMIT = 60 * 1024 * 1024
TILE = 256
CHUNK = 512

ANY = pl.BlockSpec(memory_space=pl.ANY)
SMEM = pl.BlockSpec(memory_space=pltpu.SMEM)


def swap(value, axis, bit):
    return lax.ppermute(value, axis, [(i, i ^ bit) for i in range(lax.axis_size(axis))])


def bits_of(count):
    return [1 << b for b in reversed(range(count.bit_length() - 1))]


def plus(a, b):
    return (a.astype(F32) + b.astype(F32)).astype(BF16)


def wide(a, b):
    return a.astype(F32) + b.astype(F32)


def dot(a, b, ca=1, cb=0):
    return lax.dot_general(a, b, (((ca,), (cb,)), ((), ())), preferred_element_type=F32)


def shape(*dims):
    return jax.ShapeDtypeStruct(dims, BF16)


def block(index, size):
    return pl.ds(pl.multiple_of(index * size, size), size)


class Copies:
    def __init__(self, sems):
        self.sems = sems
        self.count = 0

    def start(self, src, dst):
        copy = pltpu.make_async_copy(src, dst, self.sems.at[self.count])
        self.count += 1
        copy.start()
        return copy


def wait(copies):
    for copy in copies:
        copy.wait()


def join(arrays, fresh=()):
    n = len(arrays)
    sources, shapes = [], []
    for parts in fresh:
        rows = 0
        for array, first, count, turned in parts:
            if not any(array is x for x in [*arrays, *sources]):
                sources.append(array)
            rows += count
        tail = array.shape[1:][::-1] if turned else array.shape[1:]
        shapes.append(jax.ShapeDtypeStruct((rows, *tail), array.dtype))
    parts = [(i, *p) for i, ps in enumerate(fresh) for p in ps]

    def body(*refs):
        ins = refs[: n + len(sources)]
        outs = refs[len(ins) + n : len(ins) + n + len(fresh)]
        held = refs[len(ins) + n + len(fresh) : -1]
        copies = Copies(refs[-1])
        loads, at = [], {}
        for slot, (i, array, first, count, turned) in zip(held, parts):
            index = next(j for j, x in enumerate([*arrays, *sources]) if x is array)
            loads.append(copies.start(ins[index].at[pl.ds(first, count)], slot))
        wait(loads)
        stores, turns = [], list(held[len(parts) :])
        for slot, (i, array, first, count, turned) in zip(held, parts):
            start = at.get(i, 0)
            at[i] = start + count
            dst = outs[i].at[pl.ds(start, count)]
            if turned:
                turn = turns.pop(0)
                for k in range(count):
                    turn[k] = slot[k].T
                slot = turn
            stores.append(copies.start(slot, dst))
        wait(stores)

    turned = [(c, *a.shape[1:][::-1]) for _, a, _, c, t in parts if t]
    return pl.pallas_call(
        body,
        name="join",
        in_specs=[ANY] * (n + len(sources)),
        out_specs=[ANY] * (n + len(fresh)),
        out_shape=[jax.ShapeDtypeStruct(a.shape, a.dtype) for a in arrays] + shapes,
        input_output_aliases={i: i for i in range(n)},
        scratch_shapes=[pltpu.VMEM((p[3], *p[1].shape[1:]), p[1].dtype) for p in parts]
        + [pltpu.VMEM(dims, BF16) for dims in turned]
        + [pltpu.SemaphoreType.DMA((2 * len(parts) + 1,))],
    )(*arrays, *sources)


def prepare_body(tokens, out_grad, weight_in, weight_out, both, grads, shards, turned, wi, wo, *held):
    rows, wo_t, sems = held[0], held[1], held[-1]
    local = tokens.shape[0]
    copies = Copies(sems)
    loads = [
        copies.start(weight_out, wo),
        copies.start(tokens, rows.at[pl.ds(0, local)]),
        copies.start(out_grad, rows.at[pl.ds(local, local)]),
        copies.start(weight_in, wi),
    ]
    loads[0].wait()
    wo_t[0] = wo[0].T
    stores = [copies.start(wo_t, turned), copies.start(wo_t, shards.at[pl.ds(1, 1)])]
    wait(loads[1:])
    stores.append(copies.start(rows, both))
    stores.append(copies.start(rows.at[pl.ds(local, local)], grads))
    stores.append(copies.start(wi, shards.at[pl.ds(0, 1)]))
    wait(stores)


def prepare(tokens, out_grad, weight_in, weight_out):
    local, width = tokens.shape
    turned = weight_in.shape
    return pl.pallas_call(
        prepare_body,
        name="prepare",
        in_specs=[ANY] * 4,
        out_specs=[ANY] * 4,
        out_shape=[
            shape(2 * local, width),
            shape(local, width),
            shape(2, *turned[1:]),
            shape(*turned),
        ],
        scratch_shapes=[
            pltpu.VMEM(weight_in.shape, BF16),
            pltpu.VMEM(weight_out.shape, BF16),
            pltpu.VMEM((2 * local, width), BF16),
            pltpu.VMEM(turned, BF16),
            pltpu.SemaphoreType.DMA((9,)),
        ],
    )(tokens, out_grad, weight_in, weight_out)


def start_rows(copies, blocks, dst, local):
    return [
        copies.start(ref.at[pl.ds(first, local)], dst.at[pl.ds(i * local, local)])
        for i, (ref, first) in enumerate(blocks)
    ]


def start_weights(copies, pieces, me_d, dst, expert):
    depth = dst.shape[1] // (len(pieces) // 2)
    return [
        copies.start(ref.at[index], dst.at[s, block(me_d ^ m, depth)])
        for (s, m), (ref, index) in sorted(pieces.items())
        if s == expert
    ]


def forward_body(firsts, places, *refs):
    place, refs = refs[0], refs[1:]
    tok, refs = list(zip(refs, firsts)), refs[len(firsts) :]
    count = 1 + max(i for i, _ in places.values())
    pieces = {k: (refs[i], j) for k, (i, j) in places.items()}
    refs = refs[count:]
    act_out, slope_out, t, w, act, slope, sems = refs
    copies = Copies(sems)
    rows_in = start_rows(copies, tok, t, t.shape[0] // len(firsts))
    weights_in = [start_weights(copies, pieces, place[1], w, s) for s in range(2)]
    rows, hidden = t.shape[0], w.shape[2]
    chunk = min(CHUNK, rows)
    wait(rows_in)
    outs = []
    for s in range(2):
        wait(weights_in[s])

        @pl.loop(0, rows // chunk)
        def _(r, s=s):
            some = block(r, chunk)

            @pl.loop(0, hidden // TILE)
            def _(j):
                at = block(j, TILE)
                preact = dot(t[some, :], w[s, :, at])
                logistic = jax.nn.sigmoid(preact)
                act[s, some, at] = (preact * logistic).astype(BF16)
                slope[s, some, at] = (logistic * (1.0 + preact * (1.0 - logistic))).astype(BF16)

        outs.append(copies.start(act.at[s], act_out.at[s]))
        outs.append(copies.start(slope.at[s], slope_out.at[s]))
    wait(outs)


def backward_body(cfg, names, *refs):
    ref = dict(zip(names, refs))
    place = ref["place"]
    me_e, me_d = place[0], place[1]
    local, blocks, share = cfg["local"], cfg["blocks"], cfg["share"]
    pre, act = ref["s_pre"], ref["s_act"]
    hidden = pre.shape[2]
    copies = Copies(ref["sems"])
    g = ref.get("s_g")
    t = ref.get("s_t")
    first = []
    need = {0: [], 1: []}
    later = []
    if cfg["back"]:
        start, count = cfg["back"]
        fresh = range(start // local, (start + count) // local)
        gate, wo, table = ref["s_gate"], ref["s_wo"], ref["s_table"]
        for i in fresh:
            src = ref["grd", i].at[pl.ds(cfg["grd"][i], local)]
            first.append(copies.start(src, g.at[pl.ds(i * local, local)]))
            at = pl.ds(i * local - start, local)
            src = ref["gate", i].at[pl.ds(cfg["gate"][i], local)]
            first.append(copies.start(src, gate.at[at]))
        some = pl.ds(start, count)
        for s in (1, 0):
            pieces = {k: (ref["out", i], j) for k, (i, j) in cfg["out_places"].items()}
            need[s] += start_weights(copies, pieces, me_d, wo, s)
            need[s].append(copies.start(ref["act"].at[s, some], act.at[s, some]))
            need[s].append(copies.start(ref["pre"].at[s, some], pre.at[s, some]))
    else:
        fresh = ()
    if cfg["ins"]:
        later += start_rows(copies, [(ref["tok", i], cfg["tok"][i]) for i in range(blocks)], t, local)
    route_in = []
    if cfg["route"]:
        pieces = {k: (ref["in", i], j) for k, (i, j) in cfg["in_places"].items()}
        route_in = [c for s in range(2) for c in start_weights(copies, pieces, me_d, ref["s_wi"], s)]
    outs = []

    if cfg["back"]:
        start, count = cfg["back"]
        chunk = min(CHUNK, count) if count % min(CHUNK, count) == 0 else local
        gate_lanes = lax.broadcasted_iota(jnp.int32, (chunk, gate.shape[1]), 1)
        wait(first)
        for s in (1, 0):
            wait(need[s])

            @pl.loop(0, count // chunk)
            def _(r, s=s):
                here = block(r, chunk)
                some = pl.ds(pl.multiple_of(start + r * chunk, local), chunk)
                mine = gate_lanes == me_e ^ (share * s)
                weight = jnp.where(mine, gate[here, :].astype(F32), 0.0)
                weight = jnp.sum(weight, axis=1, keepdims=True)

                def step(j, total):
                    at = block(j, TILE)
                    back = dot(g[some, :], wo[s, :, at])
                    value = act[s, some, at].astype(F32)
                    pre[s, some, at] = (weight * pre[s, some, at].astype(F32) * back).astype(BF16)
                    act[s, some, at] = (weight * value).astype(BF16)
                    return total + jnp.sum(value * back, axis=1, keepdims=True)

                column = lax.fori_loop(0, hidden // TILE, step, jnp.zeros((chunk, 1), F32))
                column = jnp.where(mine, column, 0.0).astype(BF16)
                table[here, :] = column if s else table[here, :] + column

        outs.append(copies.start(table, ref["table_out"]))
    wait(later)

    for s in cfg["outs"]:
        stage = ref["s_out"].at[s]
        half, depth = stage.shape[1], stage.shape[3]

        @pl.loop(0, half)
        def _(j, s=s):
            for core in (1, 0):
                at = block(me_d ^ (2 * j + core), depth)
                stage[core, j] = dot(act[s], g[:, at], 0, 0).astype(BF16)

        for core in (1, 0):
            outs.append(copies.start(stage.at[core], ref["out_out", s, core]))

    for high in cfg["ins"]:
        stage = ref["s_in"].at[high]
        n, depth = stage.shape[2:4]

        @pl.loop(0, n)
        def _(j, high=high):
            for core in (1, 0):
                at = block(me_d ^ (2 * (high * n + j) + core), depth)
                for s in range(2):
                    stage[core, s, j] = dot(t[:, at], pre[s], 0, 0).astype(BF16)

        for core in (1, 0):
            outs.append(copies.start(stage.at[core], ref["in_out", high, core]))

    wait(route_in)
    for i in cfg["route"]:
        wi = ref["s_wi"]
        result = ref["s_route"]
        width = result.shape[1]

        @pl.loop(0, width // CHUNK)
        def _(j, i=i):
            at = block(j, CHUNK)
            some = pl.ds(i * local, local)
            total = dot(pre[0, some, :], wi[0, at, :], 1, 1)
            total += dot(pre[1, some, :], wi[1, at, :], 1, 1)
            result[some, at] = total.astype(BF16)

        outs.append(copies.start(result.at[pl.ds(i * local, local)], ref["route_out", i]))
    wait(outs)


def backward_call(cfg, place, held, sizes):
    rows, width, hidden, depth, experts, half = sizes
    local, blocks = cfg["local"], cfg["blocks"]
    wanted, results, scratch = ["place", "pre", "act"], {}, {}
    scratch["s_pre"] = scratch["s_act"] = (2, rows, hidden)
    taken = []
    if cfg["back"]:
        count = cfg["back"][1]
        taken = list(range(cfg["back"][0] // local, sum(cfg["back"]) // local))
        wanted += [("gate", i) for i in taken] + [k for k in held if k[0] == "out"]
        results["table_out"] = scratch["s_table"] = scratch["s_gate"] = (count, experts)
        scratch["s_wo"] = (2, width, hidden)
    if cfg["back"] or cfg["outs"]:
        scratch["s_g"] = (rows, width)
    if cfg["outs"]:
        taken = range(blocks)
        scratch["s_out"] = (2, 2, half, hidden, depth)
        for s in range(2):
            for core in range(2):
                results["out_out", s, core] = scratch["s_out"][2:]
    wanted += [("grd", i) for i in taken]
    if cfg["ins"]:
        wanted += [("tok", i) for i in range(blocks)]
        scratch["s_t"] = (rows, width)
        scratch["s_in"] = (2, 2, 2, half // 2, depth, hidden)
        for high in range(2):
            for core in range(2):
                results["in_out", high, core] = scratch["s_in"][2:]
    if cfg["route"]:
        wanted += [k for k in held if k[0] == "in"]
        scratch["s_wi"] = (2, width, hidden)
        scratch["s_route"] = (rows, width)
        for i in cfg["route"]:
            results["route_out", i] = (local, width)
    names = wanted + list(results) + list(scratch) + ["sems"]
    values = [held[k] for k in wanted[1:]]
    outs = pl.pallas_call(
        functools.partial(backward_body, cfg, names),
        name=cfg["name"],
        in_specs=[SMEM] + [ANY] * len(values),
        out_specs=[ANY] * len(results),
        out_shape=[shape(*dims) for dims in results.values()],
        scratch_shapes=[pltpu.VMEM(dims, BF16) for dims in scratch.values()]
        + [pltpu.SemaphoreType.DMA((2 * len(names) + 4 * blocks,))],
        compiler_params=pltpu.CompilerParams(vmem_limit_bytes=VMEM_LIMIT),
        cost_estimate=pl.CostEstimate(flops=0, bytes_accessed=0, transcendentals=0),
    )(place, *values)
    return dict(zip(results, outs))


def on_device(tokens, out_grad, route_ids, route_gates, weight_in, weight_out):
    local, width = tokens.shape
    experts = lax.axis_size("expert")
    slices = lax.axis_size("dp")
    hidden, depth = weight_in.shape[2], weight_in.shape[1]
    place = jnp.stack([lax.axis_index("expert"), lax.axis_index("dp")]).astype(jnp.int32)

    share = experts // 4
    token_bits = [b for b in bits_of(experts) if b != share]
    dp_bits = bits_of(slices)
    core, others = dp_bits[-1], dp_bits[:-1]

    chosen = route_ids[:, :, None] == jnp.arange(experts, dtype=jnp.int32)
    table = jnp.sum(jnp.where(chosen, route_gates.astype(F32)[:, :, None], 0.0), axis=1).astype(BF16)

    top, rest = token_bits[0], token_bits[1:]
    both, grads, shards, turned = prepare(tokens, out_grad, weight_in, weight_out)
    held = {"tok": tokens, "both": both, "grd": grads, "in": weight_in, "w": shards, "out": turned}
    held["gate"] = table
    tok, grd, gates = {0: "tok"}, {}, {0: "gate"}
    ops = []

    def op(stage, target, source, axis, bit):
        ops.append((stage, target, source, axis, bit))

    for m in range(1, experts):
        low = m & -m
        p = len([b for b in rest if b & m])
        if m & share:
            continue
        if not m & top:
            op(p - 1, ("both", m), ("both", m ^ low) if m ^ low else "both", "expert", low)
        elif m == top:
            op(0, ("tok", m), "tok", "expert", top)
            op(1, ("grd", m), "grd", "expert", top)
            op(0, ("gate", m), "gate", "expert", top)
        else:
            op(p, ("tok", m), ("tok", m ^ low), "expert", low)
            op(p + 1, ("grd", m), ("grd", m ^ low), "expert", low)
    op(0, ("in", 0), "in", "expert", share)
    op(1, ("out", 0), "out", "expert", share)
    for m in range(0, slices, 2):
        low = m & -m
        q = len([b for b in others if b & m])
        if m:
            op(q - 1, ("w", m), ("w", m ^ low) if m ^ low else "w", "dp", low)
            op(q, ("in", m), ("in", m ^ low), "dp", low)
            op(q + 1, ("out", m), ("out", m ^ low), "dp", low)
        op(q, ("w", m | core), ("w", m) if m else "w", "dp", core)
    order = [m for m in range(experts) if not m & share]
    blocks = len(order)
    rows = blocks * local
    half = slices // 2
    sizes = (rows, width, hidden, depth, experts, half)
    keys = [(s, m) for s in range(2) for m in range(slices)]
    pieces = {}
    for m in range(slices):
        for i, kind in enumerate(("in", "out")):
            pieces[kind, 0, m] = (("w", m) if m else "w", i)

    def arrays_of(where):
        names = sorted({name for name, _ in where.values()}, key=str)
        return [held[n] for n in names], {k: (names.index(n), i) for k, (n, i) in where.items()}

    def tok_place(m):
        if m & top or not m:
            return (("tok", m) if m else "tok", 0)
        return (("both", m), 0)

    def grd_place(m):
        if m & top or not m:
            return (("grd", m) if m else "grd", 0)
        return (("both", m), local)

    def forward():
        arrays, at = arrays_of({k[1:]: v for k, v in pieces.items() if k[0] == "in"})
        where = [tok_place(m) for m in order]
        return pl.pallas_call(
            functools.partial(forward_body, [first for _, first in where], at),
            name="forward",
            in_specs=[SMEM] + [ANY] * (blocks + len(arrays)),
            out_specs=[ANY] * 2,
            out_shape=[shape(2, rows, hidden)] * 2,
            scratch_shapes=[
                pltpu.VMEM((rows, width), BF16),
                pltpu.VMEM((2, width, hidden), BF16),
                pltpu.VMEM((2, rows, hidden), BF16),
                pltpu.VMEM((2, rows, hidden), BF16),
                pltpu.SemaphoreType.DMA((blocks + len(at) + 4,)),
            ],
            compiler_params=pltpu.CompilerParams(vmem_limit_bytes=VMEM_LIMIT),
            cost_estimate=pl.CostEstimate(
                flops=4 * rows * width * hidden,
                bytes_accessed=16 * rows * width + 8 * width * hidden,
                transcendentals=0,
            ),
        )(place, *[held[name] for name, _ in where], *arrays)

    last = max(o[0] for o in ops) + 1
    unsent = {(kind, m) for kind in ("in", "out") for m in range(0, slices, 2)}
    gate_where = {0: ("gate", 0)}
    number = 0
    while number <= last or unsent or rest:
        new, pack, bit = [], [], None
        if number:
            passed = [o[1] for o in ops if o[0] == number - 1]
            passed += [k for k in ("pack", "gates") if k in held]
            passed += [k for k in ("grd", "out") if number == 1]
            passed += [k for k in ("act", "pre") if k in held]
            wanted = {o[2] for o in ops if o[0] == number and isinstance(o[2], tuple)}
            passed += [k for k in sorted(wanted, key=str) if k not in passed]
            if number > 1:
                pack = [k for k in sorted(unsent) if k in held]
                unsent -= set(pack)
            if pack:
                new.append([(held[k], 0, 1, False) for k in pack])
            if number > 1 and rest:
                bit, rest = rest[0], rest[1:]
                gate_where[top] = (("gate", top), 0)
                known = sorted(gate_where)
                new.append([(held[n], i, local, False) for n, i in (gate_where[m] for m in known)])
            values = list(join([held[k] for k in passed], new))
            held.update(zip(passed, values))
            new = values[len(passed) :]
        for stage, target, source, axis, b in ops:
            if stage == number:
                held[target] = swap(held[source], axis, b)
        held.pop("pack", None)
        held.pop("gates", None)
        if pack:
            name = ("pack", number)
            held[name] = new.pop(0)
            held[name, core] = swap(held[name], "dp", core)
            for i, (kind, m) in enumerate(pack):
                pieces[kind, 1, m] = ((kind, m), 0)
                pieces[kind, 1, m | core] = ((name, core), i)
        if bit:
            name = ("gates", number)
            held[name] = swap(new.pop(0), "expert", bit)
            for i, m in enumerate(known):
                gate_where[m | bit] = (name, i * local)
        ready = all(("in", s, m) in pieces for s, m in keys)
        ready = ready and all(o[1] in held for o in ops if o[1][0] in ("tok", "both"))
        if ready and "act" not in held:
            held["act"], held["pre"] = forward()
        number += 1

    held["grd"] = out_grad
    named = {"act": held["act"], "pre": held["pre"]}
    cfg = dict(name="backward", local=local, blocks=blocks, share=share)
    cfg.update(back=(0, rows), ins=[1, 0], outs=[1, 0], route=range(blocks))
    for kind in ("in", "out"):
        arrays, cfg[kind + "_places"] = arrays_of({k[1:]: v for k, v in pieces.items() if k[0] == kind})
        named.update({(kind, i): x for i, x in enumerate(arrays)})
    for kind, where in (("tok", tok_place), ("grd", grd_place), ("gate", gate_where.get)):
        cfg[kind] = []
        for i, m in enumerate(order):
            name, first = where(m)
            named[kind, i] = held[name]
            cfg[kind].append(first)
    part = backward_call(cfg, place, named, sizes)
    route = {m: part["route_out", i] for i, m in enumerate(order)}
    (near_keep, near_send), (far_keep, far_send) = (
        [part["out_out", s, c] for c in range(2)] for s in range(2)
    )
    (low_keep, low_send), (high_keep, high_send) = (
        [part["in_out", h, c] for c in range(2)] for h in range(2)
    )
    home = part["table_out"]

    low_bit = token_bits[-1]
    out_far = plus(far_keep, swap(far_send, "dp", core))
    in_far = plus(high_keep, swap(high_send, "dp", core))

    def gates_step(bit):
        sent = [m for m in sorted(home) if m & bit]
        came = swap(jnp.concatenate([home.pop(m) for m in sent], axis=0), "expert", bit)
        for m, one in zip(sent, jnp.split(came, len(sent), axis=0)):
            home[m ^ bit] = plus(home[m ^ bit], one)

    moved = [m for m in sorted(route, reverse=True) if m & low_bit and m != low_bit]
    values = join([out_far, in_far, near_send, low_send] + [route[m] for m in moved])
    out_far, in_far, near_send, low_send = values[:4]
    route.update(zip(moved, values[4:]))
    out_came = swap(out_far, "expert", share)
    in_came = swap(in_far, "dp", others[0])
    near_sum = plus(near_keep, swap(near_send, "dp", core))
    low_sum = plus(low_keep, swap(low_send, "dp", core))
    owned = {}
    for bit in reversed(token_bits[1:]):
        for m in sorted(route, reverse=True):
            if m == bit:
                owned[m] = route.pop(m)
            elif m & bit:
                route[m ^ bit] = plus(route[m ^ bit], swap(route.pop(m), "expert", bit))
    sent = list(owned)
    values = join([route[top], home, near_sum, low_sum, *owned.values()])
    route[top], home, near_sum, low_sum = values[:4]
    owned = {m: swap(v, "expert", m) for m, v in zip(sent, values[4:])}
    owned[top] = swap(route[top], "expert", top)
    home = dict(zip(order, jnp.split(home, blocks, axis=0)))
    for bit in reversed(token_bits):
        gates_step(bit)
    total = route[0].astype(F32)
    for came in owned.values():
        total += came.astype(F32)
    grad_tokens = total.astype(BF16)
    grad_gates = jnp.sum(jnp.where(chosen, home[0].astype(F32)[:, None, :], 0.0), axis=2)

    in_sum = plus(low_sum, in_came)
    for bit in others[1:]:
        n = in_sum.shape[1] // 2
        in_sum = plus(in_sum[:, :n], swap(in_sum[:, n:], "dp", bit))
    grad_in = wide(in_sum[0, 0], swap(in_sum[1, 0], "expert", share))

    out_sum = plus(near_sum, out_came)
    for bit in others:
        n = out_sum.shape[0] // 2
        total = wide if bit == others[-1] else plus
        out_sum = total(out_sum[:n], swap(out_sum[n:], "dp", bit))
    return (grad_tokens, grad_gates.astype(BF16), grad_in[None], out_sum)


def solution(mesh):
    return jax.shard_map(
        on_device,
        mesh=mesh,
        in_specs=(
            P(("dp", "expert"), None),
            P(("dp", "expert"), None),
            P(("dp", "expert"), None),
            P(("dp", "expert"), None),
            P("expert", "dp", None),
            P("expert", None, "dp"),
        ),
        out_specs=(
            P(("dp", "expert"), None),
            P(("dp", "expert"), None),
            P("expert", "dp", None),
            P("expert", None, "dp"),
        ),
        check_vma=False,
    )
```
